32 devices in a mesh: row: 8 (over y, x, core), col: 4 (over z).
Axes of the slice: x: 2, y: 2, z: 4, core: 2. Of those that a mesh axis runs over, the one named last changes fastest.
Arguments:
- counts: int32 [8, 4, 6, 8, 128, 128], P('row', 'col'), may hold values from 0 to 5
- block_coords: int32 [3, 8, 4, 6], P(None, 'row', 'col'), may hold values from 0 to 127, as said below
- block_count: int32 [8, 4], P('row', 'col'), may hold values from 1 to 6, as said below
- factor_a: float32 [16384, 128], P(('row', 'col')), may hold values from -0.6 to 0.6
- factor_b: float32 [8192, 128], P(('col', 'row')), may hold values from -0.6 to 0.6
- factor_c: float32 [1024, 128], replicated, may hold values from -0.6 to 0.6
Outputs:
- updated_a: float32 [16384, 128], P(('row', 'col'))
- updated_b: float32 [8192, 128], P(('col', 'row'))
The draws below stay inside these ranges and needn't reach their ends.
Inputs may be any that keep to these rules, and one draw needn't show every extreme that they name: `block_coords`: the slots of one cell name distinct blocks; the first index is below 16, the second below 16, the third below 128. `block_count`: at least one cell has all 6 slots live in every draw.
All inputs are finite; a program needn't handle non-finite values.
Results may differ from the reference program's by a relative error of at most 0.0003.
Values sent between devices are 32-bit elements; how exact they have to be, the bound alone decides.
A program may use at most 64 MiB of HBM per device.

```python
import jax
import jax.numpy as jnp
from jax import lax

R = 128
K = 1024
BS = 128
BK = 8
IBLK = 16
JBLK = 16
SLOTS = 6
STEPS = 2
I = 16384
J = 8192
N_ROW = 8
N_COL = 4


def draw_block_coords(key, part):
    depth_blocks = K // BK
    per_band = IBLK * JBLK * depth_blocks
    cell_keys = jax.random.split(key, N_ROW * N_COL)
    chosen = jax.vmap(lambda cell_key: jax.random.permutation(cell_key, per_band)[:SLOTS])(cell_keys)
    block_i = chosen // (JBLK * depth_blocks)
    block_j = chosen // depth_blocks % JBLK
    block_k = chosen % depth_blocks
    stacked = jnp.stack([block_i, block_j, block_k])
    return stacked.reshape(3, N_ROW, N_COL, SLOTS).astype(jnp.int32)


def draw_block_count(key, part):
    upper_draw = jax.random.randint(jax.random.fold_in(key, 11), (N_ROW * N_COL,), 1, SLOTS + 1)
    lower_draw = jax.random.randint(jax.random.fold_in(key, 12), (N_ROW * N_COL,), 1, SLOTS + 1)
    flattened = jnp.minimum(upper_draw, lower_draw)
    chosen = jax.random.randint(jax.random.fold_in(key, 13), (), 0, N_ROW * N_COL)
    flattened = flattened.at[chosen].set(SLOTS)
    return flattened.reshape(N_ROW, N_COL).astype(jnp.int32)


def with_ends(array, own_key, smallest, largest):
    shape = array.shape
    spot = [jax.random.randint(jax.random.fold_in(own_key, axis), (), 0, shape[axis]) for axis in range(len(shape))]
    array = array.at[tuple(spot)].set(smallest)
    longest = shape.index(max(shape))
    spot[longest] = (spot[longest] + 1) % shape[longest]
    return array.at[tuple(spot)].set(largest)


def block_scale(rng, dims, cuts, smallest, high):
    gain = 1.0
    for position, parts in cuts:
        heights = jax.random.uniform(jax.random.fold_in(jax.random.fold_in(rng, 6), position), (parts,), jnp.float32, smallest / len(cuts), high / len(cuts))
        gain = gain * jnp.repeat(jnp.exp(heights), dims[position] // parts).reshape((-1,) + (1,) * (len(dims) - 1 - position))
    return gain


def setup_inputs(seed: int = 0) -> dict:
    splits = jax.random.split(jax.random.key(seed), 7)
    counts = with_ends(jax.random.randint(splits[0], (N_ROW, N_COL, SLOTS, BK, BS, BS), 0, 6), jax.random.fold_in(splits[0], 1), 0, 5).astype(jnp.int32)
    block_coords = draw_block_coords(jax.random.fold_in(splits[6], 71), 0)
    block_count = draw_block_count(jax.random.fold_in(splits[6], 71), 0)
    factor_a = jnp.clip(jax.random.uniform(splits[3], (I, R), jnp.float32, -0.6, 0.6) * block_scale(splits[3], (I, R), ((0, 32),), -0.4, 0.0), -0.6, 0.6)
    factor_b = jnp.clip(jax.random.uniform(splits[4], (J, R), jnp.float32, -0.6, 0.6) * block_scale(splits[4], (J, R), ((0, 32),), -0.4, 0.0), -0.6, 0.6)
    factor_c = jnp.clip(jax.random.uniform(splits[5], (K, R), jnp.float32, -0.6, 0.6), -0.6, 0.6)
    return {"counts": counts, "block_coords": block_coords, "block_count": block_count, "factor_a": factor_a, "factor_b": factor_b, "factor_c": factor_c}


step_rate = 0.004
highest = lax.Precision.HIGHEST


def block_gradient(piece_a, piece_b, piece_c, observed, valid_flag):
    depth = piece_c.shape[0]
    side = piece_a.shape[0]
    rank = piece_a.shape[1]
    scaled_a = (piece_c[:, None, :] * piece_a[None, :, :]).reshape(depth * side, rank)
    model = jnp.dot(scaled_a, piece_b.T, precision=highest, preferred_element_type=jnp.float32)
    residual = (jnp.exp(model) - observed.reshape(depth * side, side).astype(jnp.float32)) * valid_flag
    scaled_b = piece_c[:, None, :] * piece_b[None, :, :]
    grad_a = jnp.einsum("kab,kbr->ar", residual.reshape(depth, side, side), scaled_b, precision=highest)
    grad_b = jnp.dot(residual.T, scaled_a, precision=highest, preferred_element_type=jnp.float32)
    return grad_a, grad_b


def gradients(factor_a, factor_b, factor_c, counts, block_coords, block_count):
    band_i = IBLK * BS
    band_j = JBLK * BS

    def visit_cell(totals, cell_index):
        total_a, total_b = totals
        row_index = (cell_index // N_COL).astype(jnp.int32)
        col_index = (cell_index % N_COL).astype(jnp.int32)
        band_a = lax.dynamic_slice_in_dim(factor_a, row_index * band_i, band_i, 0)
        band_b = lax.dynamic_slice_in_dim(factor_b, col_index * band_j, band_j, 0)

        def visit_slot(partial_value, slot_index):
            grad_a, grad_b = partial_value
            start_a = (block_coords[0, row_index, col_index, slot_index] * BS).astype(jnp.int32)
            start_b = (block_coords[1, row_index, col_index, slot_index] * BS).astype(jnp.int32)
            start_c = (block_coords[2, row_index, col_index, slot_index] * BK).astype(jnp.int32)
            valid_flag = (slot_index < block_count[row_index, col_index]).astype(jnp.float32)
            piece_a = lax.dynamic_slice_in_dim(band_a, start_a, BS, 0)
            piece_b = lax.dynamic_slice_in_dim(band_b, start_b, BS, 0)
            piece_c = lax.dynamic_slice_in_dim(factor_c, start_c, BK, 0)
            observed = counts[row_index, col_index, slot_index]
            block_a, block_b = block_gradient(piece_a, piece_b, piece_c, observed, valid_flag)
            old_a = lax.dynamic_slice_in_dim(grad_a, start_a, BS, 0)
            old_b = lax.dynamic_slice_in_dim(grad_b, start_b, BS, 0)
            grad_a = lax.dynamic_update_slice_in_dim(grad_a, old_a + block_a, start_a, 0)
            grad_b = lax.dynamic_update_slice_in_dim(grad_b, old_b + block_b, start_b, 0)
            return (grad_a, grad_b), None

        empty_a = jnp.zeros((band_i, R), jnp.float32)
        empty_b = jnp.zeros((band_j, R), jnp.float32)
        (grad_a, grad_b), unused = lax.scan(visit_slot, (empty_a, empty_b), jnp.arange(SLOTS, dtype=jnp.int32))
        old_a = lax.dynamic_slice_in_dim(total_a, row_index * band_i, band_i, 0)
        old_b = lax.dynamic_slice_in_dim(total_b, col_index * band_j, band_j, 0)
        total_a = lax.dynamic_update_slice_in_dim(total_a, old_a + grad_a, row_index * band_i, 0)
        total_b = lax.dynamic_update_slice_in_dim(total_b, old_b + grad_b, col_index * band_j, 0)
        return (total_a, total_b), None

    start = (jnp.zeros_like(factor_a), jnp.zeros_like(factor_b))
    (total_a, total_b), unused = lax.scan(visit_cell, start, jnp.arange(N_ROW * N_COL, dtype=jnp.int32))
    return total_a, total_b


def reference(counts, block_coords, block_count, factor_a, factor_b, factor_c):
    for step_index in range(STEPS):
        grad_a, grad_b = gradients(factor_a, factor_b, factor_c, counts, block_coords, block_count)
        factor_a = factor_a - step_rate * grad_a
        factor_b = factor_b - step_rate * grad_b
    return factor_a, factor_b
```

```python
import functools

import jax
import jax.numpy as jnp
from jax import lax
from jax.experimental import pallas as pl
from jax.experimental.pallas import tpu as pltpu
from jax.sharding import PartitionSpec as P

STEPS = 2
step_rate = 0.004
MESH = pl.DeviceIdType.MESH


def split(x):
    high = x.astype(jnp.bfloat16)
    return high, (x - high.astype(jnp.float32)).astype(jnp.bfloat16)


def dot(x, y, dims):
    return lax.dot_general(x, y, (dims, ((), ())), preferred_element_type=jnp.float32)


def dot3(x, y, dims):
    return dot(x[0], y[0], dims) + (dot(x[0], y[1], dims) + dot(x[1], y[0], dims))


def kernel(n_row, n_col, coords, limit_ref, a_ref, b_ref, c_ref, counts_hbm, out_a, out_b,
           counts, band_a, band_b, cur_a, cur_b, raw_a, raw_b, tag_a, tag_b, acc_a, acc_b,
           counts_sem, ra_send, ra_recv, ga_send, ga_recv, gb_send, gb_recv, rb_send, rb_recv,
           ta_send, ta_recv, tb_send, tb_recv):
    r = lax.axis_index("row")
    c = lax.axis_index("col")
    own_a = a_ref.shape[0]
    own_b = b_ref.shape[0]
    side = a_ref.shape[1]
    slots = counts_hbm.shape[0]
    depth = c_ref.shape[1]
    chips = n_row // 2
    core = lax.rem(r, 2)
    partner = r + 1 - 2 * core
    limit = limit_ref[0, 0]

    def loop(n, body):
        lax.fori_loop(0, n, lambda i, carry: (body(i), carry)[1], 0)

    def row_peer(d):
        return lax.rem(r + d, n_row)

    def col_peer(d):
        return lax.rem(c + d, n_col)

    def chip_peer(d):
        return lax.rem(r + 2 * d, n_row)

    load_counts = [
        pltpu.make_async_copy(counts_hbm.at[s], counts.at[s], counts_sem.at[s]) for s in range(slots)
    ]
    for copy in load_counts:
        copy.start()

    barrier = pltpu.get_barrier_semaphore()
    loop(n_row - 1, lambda d: pl.semaphore_signal(
        barrier, inc=1, device_id=(row_peer(d + 1), c), device_id_type=MESH))
    loop(n_col - 1, lambda d: pl.semaphore_signal(
        barrier, inc=1, device_id=(r, col_peer(d + 1)), device_id_type=MESH))

    line = lax.broadcasted_iota(jnp.int32, tag_a.shape[1:], 0)
    mine_a = jnp.full(tag_a.shape[1:], -1.0, jnp.float32)
    mine_b = mine_a
    for s in range(slots):
        live = s < limit
        mine_a = jnp.where(line == s, jnp.where(live, coords[0, s], -1).astype(jnp.float32), mine_a)
        mine_b = jnp.where(line == s, jnp.where(live, coords[1, s], -1).astype(jnp.float32), mine_b)
    tag_a[c] = mine_a
    tag_b[r] = mine_b
    pl.semaphore_wait(barrier, n_row - 1 + n_col - 1)

    def chain(buf, send, recv, side_index, o, p, lead, src=None):
        to = c + 1 if side_index == 0 else c - 1
        place = buf.at[lead + (o, p)]
        return pltpu.make_async_remote_copy(
            src_ref=place if src is None else src,
            dst_ref=place,
            send_sem=send.at[lead + (side_index, o, p)],
            recv_sem=recv.at[lead + (o, p)],
            device_id=(r, to),
            device_id_type=MESH,
        )

    def across(buf, send, recv, o, p, lead, to, k, src=None):
        place = buf.at[lead + (o, p)]
        return pltpu.make_async_remote_copy(
            src_ref=place if src is None else src,
            dst_ref=place,
            send_sem=send.at[lead + (k, p)],
            recv_sem=recv.at[lead + (o, p)],
            device_id=(to, c),
            device_id_type=MESH,
        )

    def when(condition, body):
        pl.when(condition)(body)

    def chain_send(o, side_index, make, act):
        if side_index == 0:
            when(jnp.logical_and(o >= 0, jnp.logical_and(o <= c, c < n_col - 1)), lambda: act(make(0, o)))
        else:
            when(jnp.logical_and(o <= n_col - 1, jnp.logical_and(o >= c, c > 0)), lambda: act(make(1, o)))

    def gather_a(p):
        return lambda side_index, o: chain(band_a, ga_send, ga_recv, side_index, o, p, ())

    def gather_a_own(p):
        return lambda side_index, o: chain(band_a, ga_send, ga_recv, side_index, o, p, (), a_ref.at[p])

    def start(copy):
        copy.start()

    def wait_send(copy):
        copy.wait_send()

    for p in range(own_a):
        chain_send(c, 0, gather_a_own(p), start)
        chain_send(c, 1, gather_a_own(p), start)

    def gather_b(d, p):
        return across(band_b, gb_send, gb_recv, r, p, (), row_peer(d), d - 1, b_ref.at[p])

    def tag_copy_a(o, d):
        return pltpu.make_async_remote_copy(
            src_ref=tag_a.at[o], dst_ref=tag_a.at[o], send_sem=ta_send.at[d - 1], recv_sem=ta_recv.at[o],
            device_id=(r, col_peer(d)), device_id_type=MESH)

    def tag_copy_b(o, d):
        return pltpu.make_async_remote_copy(
            src_ref=tag_b.at[o], dst_ref=tag_b.at[o], send_sem=tb_send.at[d - 1], recv_sem=tb_recv.at[o],
            device_id=(row_peer(d), c), device_id_type=MESH)

    def send_b(d):
        for p in range(own_b):
            gather_b(d + 1, p).start()

    loop(n_row - 1, send_b)
    loop(n_col - 1, lambda d: tag_copy_a(c, d + 1).start())
    loop(n_row - 1, lambda d: tag_copy_b(r, d + 1).start())
    for p in range(own_a):
        band_a[c, p] = a_ref[p]
    for p in range(own_b):
        band_b[r, p] = b_ref[p]

    def pass_on(make, recv_wait, d):
        left, right = c - d, c + d

        def from_left():
            recv_wait(left)
            chain_send(left, 0, make, start)

        def from_right():
            recv_wait(right)
            chain_send(right, 1, make, start)

        when(left >= 0, from_left)
        when(right < n_col, from_right)

    def pass_a(d):
        for p in range(own_a):
            pass_on(gather_a(p), lambda o: chain(band_a, ga_send, ga_recv, 0, o, p, ()).wait_recv(), d + 1)

    loop(n_col - 1, pass_a)

    def receive_b(d):
        for p in range(own_b):
            across(band_b, gb_send, gb_recv, row_peer(d + 1), p, (), r, 0).wait_recv()

    loop(n_row - 1, receive_b)
    loop(n_col - 1, lambda d: tag_copy_a(col_peer(d + 1), 1).wait_recv())
    loop(n_row - 1, lambda d: tag_copy_b(row_peer(d + 1), 1).wait_recv())

    def first_pieces(s):
        ia = coords[0, s]
        ib = coords[1, s]
        cur_a[s] = band_a[ia // own_a, ia % own_a]
        cur_b[s] = band_b[ib // own_b, ib % own_b]

    loop(slots, first_pieces)

    def gradients(t, s):
        piece_a = cur_a[s]
        piece_b = cur_b[s]
        piece_c = c_ref[coords[2, s]]
        flag = jnp.where(s < limit, 1.0, 0.0).astype(jnp.float32)
        scaled = (piece_c[:, None, :] * piece_a[None, :, :]).reshape(depth * side, -1)
        scaled = split(scaled)
        split_b = split(piece_b)
        model = dot3(scaled, split_b, ((1,), (1,)))
        observed = counts[s].astype(jnp.float32)
        residual = split((jnp.exp(model) - observed) * flag)
        product = dot3(residual, split_b, ((1,), (0,)))
        grad_a = jnp.sum(product.reshape(depth, side, -1) * piece_c[:, None, :], axis=0)
        grad_b = dot3(residual, scaled, ((0,), (0,)))
        if t:
            grad_a = grad_a + raw_a[t - 1, c, s]
            grad_b = grad_b + raw_b[t - 1, r, s]
        raw_a[t, c, s] = grad_a
        raw_b[t, r, s] = grad_b

    def absorb(raw, tag, acc, ids, t, o):
        tags = tag[o]
        for i, block in enumerate(ids):
            match = [tags[s:s + 1, :] == block for s in range(slots)]
            total = acc[i]
            for s in range(slots):
                total = total + jnp.where(match[s], raw[t, o, s], 0.0)
            acc[i] = total

    def step(t):
        last = t == STEPS - 1

        def spread(s):
            make = lambda side_index, o: chain(raw_a, ra_send, ra_recv, side_index, o, s, (t,))
            chain_send(c, 0, make, start)
            chain_send(c, 1, make, start)
            across(raw_b, rb_send, rb_recv, r, s, (t,), partner, chips - 1).start()
            loop(chips - 1, lambda d: across(raw_b, rb_send, rb_recv, r, s, (t,), chip_peer(d + 1), d).start())

        def one(s):
            for k in range(slots):
                if t == 0:
                    when(s == k, load_counts[k].wait)
            gradients(t, s)
            spread(s)

        loop(slots, one)
        if last:
            ids_a = [(c * own_a + p).astype(jnp.float32) for p in range(own_a)]
            ids_b = [(r * own_b + p).astype(jnp.float32) for p in range(own_b)]
        else:
            ids_a = [coords[0, s].astype(jnp.float32) for s in range(slots)]
            ids_b = [coords[1, s].astype(jnp.float32) for s in range(slots)]
        acc_a[...] = jnp.zeros_like(acc_a)
        acc_b[...] = jnp.zeros_like(acc_b)
        take_a = lambda o: absorb(raw_a, tag_a, acc_a, ids_a, t, o)
        take_b = lambda o: absorb(raw_b, tag_b, acc_b, ids_b, t, o)

        def forward(d):
            def passing(s):
                make = lambda side_index, o: chain(raw_a, ra_send, ra_recv, side_index, o, s, (t,))
                pass_on(make, lambda o: make(0, o).wait_recv(), d)
                origin = chip_peer(d)

                def hand_over():
                    across(raw_b, rb_send, rb_recv, origin, s, (t,), r, 0).wait_recv()
                    across(raw_b, rb_send, rb_recv, origin, s, (t,), partner, chips - 1 + d).start()

                when(d < chips, hand_over)

            loop(slots, passing)

        def receive_partner(d):
            origin = lax.rem(partner + 2 * d, n_row)
            for s in range(slots):
                across(raw_b, rb_send, rb_recv, origin, s, (t,), r, 0).wait_recv()

        loop(max(n_col, chips) - 1, lambda d: forward(d + 1))
        loop(chips, receive_partner)
        loop(n_col, take_a)
        loop(n_row, take_b)
        if last:
            for p in range(own_a):
                out_a[p] = a_ref[p] - step_rate * acc_a[p]
            for p in range(own_b):
                out_b[p] = b_ref[p] - step_rate * acc_b[p]
        else:
            for s in range(slots):
                cur_a[s] = cur_a[s] - step_rate * acc_a[s]
                cur_b[s] = cur_b[s] - step_rate * acc_b[s]

    for t in range(STEPS):
        step(t)

    def sent_a(o):
        for side_index in range(2):
            for p in range(own_a):
                chain_send(o, side_index, gather_a(p), wait_send)
            for t in range(STEPS):
                def sent(s):
                    make = lambda k, origin: chain(raw_a, ra_send, ra_recv, k, origin, s, (t,))
                    chain_send(o, side_index, make, wait_send)

                loop(slots, sent)

    loop(n_col, sent_a)

    def sent_b(d):
        for p in range(own_b):
            gather_b(d + 1, p).wait_send()

    loop(n_row - 1, sent_b)
    loop(n_col - 1, lambda d: tag_copy_a(c, d + 1).wait_send())
    loop(n_row - 1, lambda d: tag_copy_b(r, d + 1).wait_send())
    for t in range(STEPS):
        def sent_raw_b(k):
            for s in range(slots):
                across(raw_b, rb_send, rb_recv, r, s, (t,), partner, k).wait_send()

        loop(2 * chips - 1, sent_raw_b)


def local(n_row, n_col, counts, block_coords, block_count, factor_a, factor_b, factor_c):
    slots, depth, side = counts.shape[2:5]
    rank = factor_a.shape[1]
    own_a = factor_a.shape[0] // side
    own_b = factor_b.shape[0] // side
    chips = n_row // 2
    lines = -(-slots // 8) * 8
    f32 = jnp.float32
    vmem = pl.BlockSpec(memory_space=pltpu.VMEM)
    smem = pl.BlockSpec(memory_space=pltpu.SMEM)
    dma = pltpu.SemaphoreType.DMA
    out_a, out_b = pl.pallas_call(
        functools.partial(kernel, n_row, n_col),
        out_shape=(
            jax.ShapeDtypeStruct((own_a, side, rank), f32),
            jax.ShapeDtypeStruct((own_b, side, rank), f32),
        ),
        in_specs=[smem, smem, vmem, vmem, vmem, pl.BlockSpec(memory_space=pl.ANY)],
        out_specs=(vmem, vmem),
        scratch_shapes=[
            pltpu.VMEM((slots, depth * side, side), jnp.int32),
            pltpu.VMEM((n_col, own_a, side, rank), f32),
            pltpu.VMEM((n_row, own_b, side, rank), f32),
            pltpu.VMEM((slots, side, rank), f32),
            pltpu.VMEM((slots, side, rank), f32),
            pltpu.VMEM((STEPS, n_col, slots, side, rank), f32),
            pltpu.VMEM((STEPS, n_row, slots, side, rank), f32),
            pltpu.VMEM((n_col, lines, rank), f32),
            pltpu.VMEM((n_row, lines, rank), f32),
            pltpu.VMEM((max(slots, own_a), side, rank), f32),
            pltpu.VMEM((max(slots, own_b), side, rank), f32),
            dma((slots,)),
            dma((STEPS, 2, n_col, slots)),
            dma((STEPS, n_col, slots)),
            dma((2, n_col, own_a)),
            dma((n_col, own_a)),
            dma((n_row - 1, own_b)),
            dma((n_row, own_b)),
            dma((STEPS, 2 * chips - 1, slots)),
            dma((STEPS, n_row, slots)),
            dma((n_col - 1,)),
            dma((n_col,)),
            dma((n_row - 1,)),
            dma((n_row,)),
        ],
        compiler_params=pltpu.CompilerParams(
            collective_id=0, has_side_effects=True, vmem_limit_bytes=56 * 1024 * 1024
        ),
    )(
        block_coords.reshape(3, slots),
        block_count,
        factor_a.reshape(own_a, side, rank),
        factor_b.reshape(own_b, side, rank),
        factor_c.reshape(-1, depth, rank),
        counts.reshape(slots, depth * side, side),
    )
    return out_a.reshape(factor_a.shape), out_b.reshape(factor_b.shape)


def solution(mesh):
    n_row = mesh.shape["row"]
    n_col = mesh.shape["col"]
    return jax.shard_map(
        functools.partial(local, n_row, n_col),
        mesh=mesh,
        in_specs=(
            P("row", "col", None, None, None, None),
            P(None, "row", "col", None),
            P("row", "col"),
            P(("row", "col"), None),
            P(("col", "row"), None),
            P(),
        ),
        out_specs=(P(("row", "col"), None), P(("col", "row"), None)),
        check_vma=False,
    )
```

```python
import functools

import jax
import jax.numpy as jnp
from jax import lax
from jax.experimental import pallas as pl
from jax.experimental.pallas import tpu as pltpu
from jax.sharding import PartitionSpec as P

STEPS = 2
SLICES = 8
step_rate = 0.004
MESH = pl.DeviceIdType.MESH


def split(x):
    high = x.astype(jnp.bfloat16)
    return high, (x - high.astype(jnp.float32)).astype(jnp.bfloat16)


def dot(x, y, dims):
    return lax.dot_general(x, y, (dims, ((), ())), preferred_element_type=jnp.float32)


def dot3(x, y, dims):
    return dot(x[0], y[0], dims) + (dot(x[0], y[1], dims) + dot(x[1], y[0], dims))


def kernel(n_row, n_col, coords, limit_ref, a_ref, b_ref, c_ref, counts_hbm, out_a, out_b,
           counts, band_a, band_b, sel_out, sel_in, cur_a, cur_b, raw_a, raw_b, part_out, part_in,
           tag_a, tag_b, acc_a, acc_b,
           counts_sem, ga_send, ga_recv, sel_send, sel_recv, gb_send, gb_recv,
           own_send, own_recv, far_send, far_recv, part_send, part_recv, rb_send, rb_recv, pb_send, pb_recv,
           ta_send, ta_recv, tb_send, tb_recv):
    r = lax.axis_index("row")
    c = lax.axis_index("col")
    own_a = a_ref.shape[0]
    own_b = b_ref.shape[0]
    side = a_ref.shape[1]
    slots = counts_hbm.shape[0]
    depth = c_ref.shape[1]
    chips = n_row // 2
    core = lax.rem(r, 2)
    partner = r + 1 - 2 * core
    limit = limit_ref[0, 0]
    end = n_col - 1
    both = jnp.logical_and
    high = side // SLICES
    groups = rb_recv.shape[2]
    bunch = slots // groups

    def loop(n, body):
        lax.fori_loop(0, n, lambda i, carry: (body(i), carry)[1], 0)

    def when(condition, body):
        pl.when(condition)(body)

    def row_peer(d):
        return lax.rem(r + d, n_row)

    def col_peer(d):
        return lax.rem(c + d, n_col)

    def chip_peer(d):
        return lax.rem(r + 2 * d, n_row)

    def cut(q):
        return pl.ds(pl.multiple_of(q * high, high), high)

    def remote(src, dst, send, recv, to):
        return pltpu.make_async_remote_copy(
            src_ref=src, dst_ref=dst, send_sem=send, recv_sem=recv, device_id=to, device_id_type=MESH)

    load_counts = [
        pltpu.make_async_copy(counts_hbm.at[s], counts.at[s], counts_sem.at[s]) for s in range(slots)
    ]
    for copy in load_counts:
        copy.start()

    barrier = pltpu.get_barrier_semaphore()
    loop(n_row - 1, lambda d: pl.semaphore_signal(
        barrier, inc=1, device_id=(row_peer(d + 1), c), device_id_type=MESH))
    loop(n_col - 1, lambda d: pl.semaphore_signal(
        barrier, inc=1, device_id=(r, col_peer(d + 1)), device_id_type=MESH))

    line = lax.broadcasted_iota(jnp.int32, tag_a.shape[1:], 0)
    mine_a = jnp.full(tag_a.shape[1:], -1.0, jnp.float32)
    mine_b = mine_a
    for s in range(slots):
        live = s < limit
        mine_a = jnp.where(line == s, jnp.where(live, coords[0, 0, 0, s], -1).astype(jnp.float32), mine_a)
        mine_b = jnp.where(line == s, jnp.where(live, coords[1, 0, 0, s], -1).astype(jnp.float32), mine_b)
    tag_a[c] = mine_a
    tag_b[r] = mine_b
    for p in range(own_a):
        band_a[c, p] = a_ref[p]
    for p in range(own_b):
        band_b[r, p] = b_ref[p]
    pl.semaphore_wait(barrier, n_row - 1 + n_col - 1)

    def tag_copy_a(o, d):
        return remote(tag_a.at[o], tag_a.at[o], ta_send.at[d - 1], ta_recv.at[o], (r, col_peer(d)))

    def tag_copy_b(o, d):
        return remote(tag_b.at[o], tag_b.at[o], tb_send.at[d - 1], tb_recv.at[o], (row_peer(d), c))

    def gather_b(o, d):
        return remote(band_b.at[o], band_b.at[o], gb_send.at[d - 1], gb_recv.at[o], (row_peer(d), c))

    loop(n_col - 1, lambda d: tag_copy_a(c, d + 1).start())

    def toward(k):
        return (r, c + 1 - 2 * k)

    def is_next_to_end(k):
        return c == n_col - 2 if k == 0 else c == 1

    def passes_rows(k):
        return c < n_col - 2 if k == 0 else c > 1

    def takes_rows(k):
        return c < end if k == 0 else c > 0

    def origin_of(k, d):
        return c - d if k == 0 else c + d

    def inside(o):
        return both(o >= 0, o < n_col)

    def gather_a(k, o, q):
        place = band_a.at[o, :, cut(q)]
        return remote(place, place, ga_send.at[k, o], ga_recv.at[o, q], toward(k))

    def choose(k, q):
        targets = tag_a[c + 1 - 2 * k]
        origins = range(0, n_col - 1) if k == 0 else range(1, n_col)
        for s in range(slots):
            target = targets[s:s + 1, :]
            total = jnp.zeros((high, a_ref.shape[2]), jnp.float32)
            for o in origins:
                for p in range(own_a):
                    total = jnp.where(target == float(o * own_a + p), band_a[o, p, cut(q)], total)
            sel_out[k, s, cut(q)] = total

    def sel_copy(k, q):
        return remote(sel_out.at[k, :, cut(q)], sel_in.at[:, cut(q)], sel_send.at[k], sel_recv.at[0], toward(k))

    def gather_slice(q):
        for k in range(2):
            when(passes_rows(k), lambda: gather_a(k, c, q).start())
        for d in range(1, n_col - 1):
            for k in range(2):
                o = origin_of(k, d)

                def arrived():
                    gather_a(k, o, q).wait_recv()
                    when(passes_rows(k), lambda: gather_a(k, o, q).start())

                when(both(inside(o), takes_rows(k)), arrived)
        for k in range(2):
            def chosen():
                when(q == 0, lambda: tag_copy_a(c + 1 - 2 * k, 1).wait_recv())
                choose(k, q)
                sel_copy(k, q).start()

            when(is_next_to_end(k), chosen)

    loop(n_row - 1, lambda d: gather_b(r, d + 1).start())
    loop(n_row - 1, lambda d: tag_copy_b(r, d + 1).start())
    loop(SLICES, gather_slice)

    def receive_tag(d):
        o = col_peer(d + 1)
        taken = jnp.logical_or(
            both(is_next_to_end(0), o == c + 1), both(is_next_to_end(1), o == c - 1))
        when(jnp.logical_not(taken), lambda: tag_copy_a(o, 1).wait_recv())

    loop(n_col - 1, receive_tag)
    loop(n_row - 1, lambda d: gather_b(row_peer(d + 1), 1).wait_recv())
    loop(n_row - 1, lambda d: tag_copy_b(row_peer(d + 1), 1).wait_recv())
    at_end = jnp.logical_or(c == 0, c == end)
    when(at_end, lambda: remote(sel_in, sel_in, sel_send.at[0], sel_recv.at[0], (r, c)).wait_recv())

    def first_pieces(s):
        ia = coords[0, 0, 0, s]
        ib = coords[1, 0, 0, s]
        cur_b[s] = band_b[ib // own_b, ib % own_b]

        def from_selection():
            cur_a[s] = jnp.where(ia // own_a == c, a_ref[ia % own_a], sel_in[s])

        def from_band():
            cur_a[s] = band_a[ia // own_a, ia % own_a]

        when(at_end, from_selection)
        when(jnp.logical_not(at_end), from_band)

    loop(slots, first_pieces)

    def gradients(t, s):
        piece_a = cur_a[s]
        piece_b = cur_b[s]
        piece_c = c_ref[coords[2, 0, 0, s]]
        flag = jnp.where(s < limit, 1.0, 0.0).astype(jnp.float32)
        scaled = (piece_c[:, None, :] * piece_a[None, :, :]).reshape(depth * side, -1)
        scaled = split(scaled)
        split_b = split(piece_b)
        model = dot3(scaled, split_b, ((1,), (1,)))
        observed = counts[s].astype(jnp.float32)
        residual = split((jnp.exp(model) - observed) * flag)
        product = dot3(residual, split_b, ((1,), (0,)))
        grad_a = jnp.sum(product.reshape(depth, side, -1) * piece_c[:, None, :], axis=0)
        grad_b = dot3(residual, scaled, ((0,), (0,)))
        if t:
            grad_a = grad_a + raw_a[t - 1, c, s]
            grad_b = grad_b + raw_b[t - 1, r, s]
        raw_a[t, c, s] = grad_a
        raw_b[t, r, s] = grad_b

    def absorb(raw, tag, acc, ids, t, o):
        tags = tag[o]
        for i, block in enumerate(ids):
            match = [tags[s:s + 1, :] == block for s in range(slots)]
            total = acc[i]
            for s in range(slots):
                total = total + jnp.where(match[s], raw[t, o, s], 0.0)
            acc[i] = total

    def own_copy(t, k, o, s):
        place = raw_a.at[t, o, s]
        return remote(place, place, own_send.at[t, k], own_recv.at[t, k], toward(k))

    def own_whole(t, k, o):
        place = raw_a.at[t, o]
        return remote(place, place, own_send.at[t, k], own_recv.at[t, k], toward(k))

    def far_copy(t, k, o, q):
        place = raw_a.at[t, o, :, cut(q)]
        return remote(place, place, far_send.at[t, k, o], far_recv.at[t, o, q], toward(k))

    def wanted(t):
        return own_a if t == STEPS - 1 else slots

    def part_copy(t, k, q):
        n = wanted(t)
        return remote(part_out.at[t, k, pl.ds(0, n), cut(q)], part_in.at[t, pl.ds(0, n), cut(q)],
                      part_send.at[t, k], part_recv.at[t], toward(k))

    def part_whole(t, k):
        n = wanted(t)
        return remote(part_out.at[t, k, pl.ds(0, n)], part_in.at[t, pl.ds(0, n)],
                      part_send.at[t, k], part_recv.at[t], toward(k))

    def bunch_b(t, o, g, to, send, recv):
        place = raw_b.at[t, o, pl.ds(g * bunch, bunch)]
        return remote(place, place, send, recv, (to, c))

    def cross_send(t, s, d):
        g = s // bunch
        place = raw_b.at[t, r, s]
        return remote(place, place, rb_send.at[t, d - 1], rb_recv.at[t, r, g], (chip_peer(d), c))

    def cross_recv(t, o, g):
        return bunch_b(t, o, g, r, rb_send.at[t, 0], rb_recv.at[t, o, g])

    def pair_send(t, s):
        place = raw_b.at[t, r, s]
        return remote(place, place, pb_send.at[t, 0], pb_recv.at[t, r, s // bunch], (partner, c))

    def pair_pass(t, d, g):
        o = chip_peer(d)
        return bunch_b(t, o, g, partner, pb_send.at[t, d], pb_recv.at[t, o, g])

    def pair_recv(t, o, g):
        return bunch_b(t, o, g, r, pb_send.at[t, 0], pb_recv.at[t, o, g])

    def step(t):
        last = t == STEPS - 1

        def one(s):
            for k in range(slots):
                if t == 0:
                    when(s == k, load_counts[k].wait)
            gradients(t, s)
            when(c < end, lambda: own_copy(t, 0, c, s).start())
            when(c > 0, lambda: own_copy(t, 1, c, s).start())
            loop(chips - 1, lambda d: cross_send(t, s, d + 1).start())
            pair_send(t, s).start()

        loop(slots, one)
        if last:
            ids_a = [(c * own_a + p).astype(jnp.float32) for p in range(own_a)]
            ids_b = [(r * own_b + p).astype(jnp.float32) for p in range(own_b)]
        else:
            ids_a = [coords[0, 0, 0, s].astype(jnp.float32) for s in range(slots)]
            ids_b = [coords[1, 0, 0, s].astype(jnp.float32) for s in range(slots)]
        take_a = lambda o: absorb(raw_a, tag_a, acc_a, ids_a, t, o)
        take_b = lambda o: absorb(raw_b, tag_b, acc_b, ids_b, t, o)
        acc_a[...] = jnp.zeros_like(acc_a)
        acc_b[...] = jnp.zeros_like(acc_b)
        take_a(c)
        take_b(r)

        for k in range(2):
            o = origin_of(k, 1)

            def neighbour():
                own_whole(t, k, o).wait_recv()
                when(passes_rows(k), lambda: loop(SLICES, lambda q: far_copy(t, k, o, q).start()))

            when(inside(o), neighbour)
        for g in range(groups):
            pair_recv(t, partner, g).wait_recv()

        def part(k, q):
            there = c + 1 - 2 * k
            origins = range(0, n_col - 2) if k == 0 else range(2, n_col)
            aims = tag_a[there]
            for i in range(wanted(t)):
                if last:
                    aim = (there * own_a + i).astype(jnp.float32)
                else:
                    aim = aims[i:i + 1, :]
                total = jnp.zeros((high, a_ref.shape[2]), jnp.float32)
                for o in origins:
                    tags = tag_a[o]
                    for s in range(slots):
                        total = total + jnp.where(tags[s:s + 1, :] == aim, raw_a[t, o, s, cut(q)], 0.0)
                part_out[t, k, i, cut(q)] = total

        def far_slice(q):
            for d in range(2, n_col - 1):
                for k in range(2):
                    o = origin_of(k, d)

                    def arrived():
                        far_copy(t, k, o, q).wait_recv()
                        when(passes_rows(k), lambda: far_copy(t, k, o, q).start())

                    when(both(inside(o), takes_rows(k)), arrived)
            if n_col > 2:
                for k in range(2):
                    def summed():
                        part(k, q)
                        part_copy(t, k, q).start()

                    when(is_next_to_end(k), summed)

        loop(SLICES, far_slice)
        take_b(partner)
        for k in range(2):
            when(inside(origin_of(k, 1)), lambda: take_a(origin_of(k, 1)))

        def hand_over(d):
            for g in range(groups):
                cross_recv(t, chip_peer(d), g).wait_recv()
                pair_pass(t, d, g).start()

        loop(chips - 1, lambda d: hand_over(d + 1))
        loop(chips - 1, lambda d: take_b(chip_peer(d + 1)))

        def far_take(d):
            for k in range(2):
                o = origin_of(k, d)
                when(both(inside(o), takes_rows(k)), lambda: take_a(o))

        loop(max(n_col - 3, 0), lambda d: far_take(d + 2))
        if n_col > 2:
            def add_part():
                part_whole(t, 0).wait_recv()
                for i in range(wanted(t)):
                    acc_a[i] = acc_a[i] + part_in[t, i]

            when(at_end, add_part)

        def receive_pair(d):
            o = lax.rem(partner + 2 * d, n_row)
            for g in range(groups):
                pair_recv(t, o, g).wait_recv()
            take_b(o)

        loop(chips - 1, lambda d: receive_pair(d + 1))
        if last:
            for p in range(own_a):
                out_a[p] = a_ref[p] - step_rate * acc_a[p]
            for p in range(own_b):
                out_b[p] = b_ref[p] - step_rate * acc_b[p]
        else:
            for s in range(slots):
                cur_a[s] = cur_a[s] - step_rate * acc_a[s]
                cur_b[s] = cur_b[s] - step_rate * acc_b[s]

    for t in range(STEPS):
        step(t)

    for k in range(2):
        def sent_shard(o, k=k):
            place = band_a.at[o]
            remote(place, place, ga_send.at[k, o], ga_recv.at[o, 0], toward(k)).wait_send()

        def sent_far(t, o, k=k):
            place = raw_a.at[t, o]
            remote(place, place, far_send.at[t, k, o], far_recv.at[t, o, 0], toward(k)).wait_send()

        def sent_from(d):
            o = origin_of(k, d)
            when(both(inside(o), passes_rows(k)), lambda: sent_shard(o))

        def sent_far_from(d):
            o = origin_of(k, d)
            for t in range(STEPS):
                when(both(inside(o), passes_rows(k)), lambda: sent_far(t, o))

        loop(n_col - 1, sent_from)
        loop(n_col - 2, lambda d: sent_far_from(d + 1))
        when(is_next_to_end(k),
             lambda: remote(sel_out.at[k], sel_in, sel_send.at[k], sel_recv.at[0], toward(k)).wait_send())
        for t in range(STEPS):
            when(c < end if k == 0 else c > 0, lambda: own_whole(t, k, c).wait_send())
            if n_col > 2:
                when(is_next_to_end(k), lambda: part_whole(t, k).wait_send())
    loop(n_row - 1, lambda d: gather_b(r, d + 1).wait_send())
    loop(n_col - 1, lambda d: tag_copy_a(c, d + 1).wait_send())
    loop(n_row - 1, lambda d: tag_copy_b(r, d + 1).wait_send())
    for t in range(STEPS):
        place = raw_b.at[t, r]
        loop(chips - 1, lambda d: remote(
            place, place, rb_send.at[t, d], rb_recv.at[t, r, 0], (chip_peer(d + 1), c)).wait_send())
        loop(chips, lambda d: remote(
            place, place, pb_send.at[t, d], pb_recv.at[t, r, 0], (partner, c)).wait_send())


def local(n_row, n_col, counts, block_coords, block_count, factor_a, factor_b, factor_c):
    slots, depth, side = counts.shape[2:5]
    rank = factor_a.shape[1]
    own_a = factor_a.shape[0] // side
    own_b = factor_b.shape[0] // side
    chips = n_row // 2
    lines = -(-slots // 8) * 8
    groups = 2 if slots % 2 == 0 else 1
    most = max(slots, own_a)
    f32 = jnp.float32
    vmem = pl.BlockSpec(memory_space=pltpu.VMEM)
    smem = pl.BlockSpec(memory_space=pltpu.SMEM)
    dma = pltpu.SemaphoreType.DMA
    out_a, out_b = pl.pallas_call(
        functools.partial(kernel, n_row, n_col),
        out_shape=(
            jax.ShapeDtypeStruct((own_a, side, rank), f32),
            jax.ShapeDtypeStruct((own_b, side, rank), f32),
        ),
        in_specs=[smem, smem, vmem, vmem, vmem, pl.BlockSpec(memory_space=pl.ANY)],
        out_specs=(vmem, vmem),
        scratch_shapes=[
            pltpu.VMEM((slots, depth * side, side), jnp.int32),
            pltpu.VMEM((n_col, own_a, side, rank), f32),
            pltpu.VMEM((n_row, own_b, side, rank), f32),
            pltpu.VMEM((2, slots, side, rank), f32),
            pltpu.VMEM((slots, side, rank), f32),
            pltpu.VMEM((slots, side, rank), f32),
            pltpu.VMEM((slots, side, rank), f32),
            pltpu.VMEM((STEPS, n_col, slots, side, rank), f32),
            pltpu.VMEM((STEPS, n_row, slots, side, rank), f32),
            pltpu.VMEM((STEPS, 2, most, side, rank), f32),
            pltpu.VMEM((STEPS, most, side, rank), f32),
            pltpu.VMEM((n_col, lines, rank), f32),
            pltpu.VMEM((n_row, lines, rank), f32),
            pltpu.VMEM((most, side, rank), f32),
            pltpu.VMEM((max(slots, own_b), side, rank), f32),
            dma((slots,)),
            dma((2, n_col)),
            dma((n_col, SLICES)),
            dma((2,)),
            dma((1,)),
            dma((n_row - 1,)),
            dma((n_row,)),
            dma((STEPS, 2)),
            dma((STEPS, 2)),
            dma((STEPS, 2, n_col)),
            dma((STEPS, n_col, SLICES)),
            dma((STEPS, 2)),
            dma((STEPS,)),
            dma((STEPS, chips - 1)),
            dma((STEPS, n_row, groups)),
            dma((STEPS, chips)),
            dma((STEPS, n_row, groups)),
            dma((n_col - 1,)),
            dma((n_col,)),
            dma((n_row - 1,)),
            dma((n_row,)),
        ],
        compiler_params=pltpu.CompilerParams(
            collective_id=0, has_side_effects=True, vmem_limit_bytes=56 * 1024 * 1024
        ),
    )(
        block_coords,
        block_count,
        factor_a.reshape(own_a, side, rank),
        factor_b.reshape(own_b, side, rank),
        factor_c.reshape(-1, depth, rank),
        counts.reshape(slots, depth * side, side),
    )
    return out_a.reshape(factor_a.shape), out_b.reshape(factor_b.shape)


def solution(mesh):
    n_row = mesh.shape["row"]
    n_col = mesh.shape["col"]
    return jax.shard_map(
        functools.partial(local, n_row, n_col),
        mesh=mesh,
        in_specs=(
            P("row", "col", None, None, None, None),
            P(None, "row", "col", None),
            P("row", "col"),
            P(("row", "col"), None),
            P(("col", "row"), None),
            P(),
        ),
        out_specs=(P(("row", "col"), None), P(("col", "row"), None)),
        check_vma=False,
    )
```

```python
import functools

import jax
import jax.numpy as jnp
from jax import lax
from jax.experimental import pallas as pl
from jax.experimental.pallas import tpu as pltpu
from jax.sharding import PartitionSpec as P

STEPS = 2
SLICES = 2
step_rate = 0.004
MESH = pl.DeviceIdType.MESH


def split(x):
    high = x.astype(jnp.bfloat16)
    return high, (x - high.astype(jnp.float32)).astype(jnp.bfloat16)


def dot(x, y, dims):
    return lax.dot_general(x, y, (dims, ((), ())), preferred_element_type=jnp.float32)


def dot3(x, y, dims):
    return dot(x[0], y[0], dims) + (dot(x[0], y[1], dims) + dot(x[1], y[0], dims))


def kernel(n_row, n_col, coords, limit_ref, a_ref, b_ref, c_ref, counts_hbm, out_a, out_b,
           counts, band_a, band_b, sel_out, sel_in, cur_a, cur_b, raw_a, raw_b, part_out, part_in,
           tag_a, tag_b, acc_a, acc_b,
           counts_sem, ga_send, ga_recv, sel_send, sel_recv, gb_send, gb_recv,
           own_send, own_recv, far_send, far_recv, part_send, part_recv, rb_send, rb_recv, pb_send, pb_recv,
           ta_send, ta_recv, tb_send, tb_recv):
    r = lax.axis_index("row")
    c = lax.axis_index("col")
    own_a = a_ref.shape[0]
    own_b = b_ref.shape[0]
    side = a_ref.shape[1]
    slots = counts_hbm.shape[0]
    depth = c_ref.shape[1]
    chips = n_row // 2
    core = lax.rem(r, 2)
    partner = r + 1 - 2 * core
    limit = limit_ref[0, 0]
    end = n_col - 1
    both = jnp.logical_and
    high = side // SLICES
    groups = rb_recv.shape[2]
    bunch = slots // groups

    def loop(n, body):
        lax.fori_loop(0, n, lambda i, carry: (body(i), carry)[1], 0)

    def when(condition, body):
        pl.when(condition)(body)

    def row_peer(d):
        return lax.rem(r + d, n_row)

    def col_peer(d):
        return lax.rem(c + d, n_col)

    def chip_peer(d):
        return lax.rem(r + 2 * d, n_row)

    def cut(q):
        return pl.ds(pl.multiple_of(q * high, high), high)

    def remote(src, dst, send, recv, to):
        return pltpu.make_async_remote_copy(
            src_ref=src, dst_ref=dst, send_sem=send, recv_sem=recv, device_id=to, device_id_type=MESH)

    load_counts = [
        pltpu.make_async_copy(counts_hbm.at[s], counts.at[s], counts_sem.at[s]) for s in range(slots)
    ]
    for copy in load_counts:
        copy.start()

    barrier = pltpu.get_barrier_semaphore()
    loop(n_row - 1, lambda d: pl.semaphore_signal(
        barrier, inc=1, device_id=(row_peer(d + 1), c), device_id_type=MESH))
    loop(n_col - 1, lambda d: pl.semaphore_signal(
        barrier, inc=1, device_id=(r, col_peer(d + 1)), device_id_type=MESH))

    line = lax.broadcasted_iota(jnp.int32, tag_a.shape[1:], 0)
    mine_a = jnp.full(tag_a.shape[1:], -1.0, jnp.float32)
    mine_b = mine_a
    for s in range(slots):
        live = s < limit
        mine_a = jnp.where(line == s, jnp.where(live, coords[0, 0, 0, s], -1).astype(jnp.float32), mine_a)
        mine_b = jnp.where(line == s, jnp.where(live, coords[1, 0, 0, s], -1).astype(jnp.float32), mine_b)
    tag_a[c] = mine_a
    tag_b[r] = mine_b
    for p in range(own_a):
        band_a[c, p] = a_ref[p]
    for p in range(own_b):
        band_b[r, p] = b_ref[p]
    pl.semaphore_wait(barrier, n_row - 1 + n_col - 1)

    def tag_copy_a(o, d):
        return remote(tag_a.at[o], tag_a.at[o], ta_send.at[d - 1], ta_recv.at[o], (r, col_peer(d)))

    def tag_copy_b(o, d):
        return remote(tag_b.at[o], tag_b.at[o], tb_send.at[d - 1], tb_recv.at[o], (row_peer(d), c))

    def gather_b(o, d):
        return remote(band_b.at[o], band_b.at[o], gb_send.at[d - 1], gb_recv.at[o], (row_peer(d), c))

    loop(n_col - 1, lambda d: tag_copy_a(c, d + 1).start())

    def toward(k):
        return (r, c + 1 - 2 * k)

    def is_next_to_end(k):
        return c == n_col - 2 if k == 0 else c == 1

    def passes_rows(k):
        return c < n_col - 2 if k == 0 else c > 1

    def takes_rows(k):
        return c < end if k == 0 else c > 0

    def origin_of(k, d):
        return c - d if k == 0 else c + d

    def inside(o):
        return both(o >= 0, o < n_col)

    def gather_a(k, o, q):
        place = band_a.at[o, :, cut(q)]
        return remote(place, place, ga_send.at[k, o], ga_recv.at[o, q], toward(k))

    def choose(k, q):
        targets = tag_a[c + 1 - 2 * k]
        origins = range(0, n_col - 1) if k == 0 else range(1, n_col)
        for s in range(slots):
            target = targets[s:s + 1, :]
            total = jnp.zeros((high, a_ref.shape[2]), jnp.float32)
            for o in origins:
                for p in range(own_a):
                    total = jnp.where(target == float(o * own_a + p), band_a[o, p, cut(q)], total)
            sel_out[k, s, cut(q)] = total

    def sel_copy(k, q):
        return remote(sel_out.at[k, :, cut(q)], sel_in.at[:, cut(q)], sel_send.at[k], sel_recv.at[0], toward(k))

    def gather_slice(q):
        for k in range(2):
            when(passes_rows(k), lambda: gather_a(k, c, q).start())
        for d in range(1, n_col - 1):
            for k in range(2):
                o = origin_of(k, d)

                def arrived():
                    gather_a(k, o, q).wait_recv()
                    when(passes_rows(k), lambda: gather_a(k, o, q).start())

                when(both(inside(o), takes_rows(k)), arrived)
        for k in range(2):
            def chosen():
                when(q == 0, lambda: tag_copy_a(c + 1 - 2 * k, 1).wait_recv())
                choose(k, q)
                sel_copy(k, q).start()

            when(is_next_to_end(k), chosen)

    loop(n_row - 1, lambda d: gather_b(r, d + 1).start())
    loop(n_row - 1, lambda d: tag_copy_b(r, d + 1).start())
    loop(SLICES, gather_slice)

    def receive_tag(d):
        o = col_peer(d + 1)
        taken = jnp.logical_or(
            both(is_next_to_end(0), o == c + 1), both(is_next_to_end(1), o == c - 1))
        when(jnp.logical_not(taken), lambda: tag_copy_a(o, 1).wait_recv())

    loop(n_col - 1, receive_tag)
    loop(n_row - 1, lambda d: gather_b(row_peer(d + 1), 1).wait_recv())
    loop(n_row - 1, lambda d: tag_copy_b(row_peer(d + 1), 1).wait_recv())
    at_end = jnp.logical_or(c == 0, c == end)
    when(at_end, lambda: remote(sel_in, sel_in, sel_send.at[0], sel_recv.at[0], (r, c)).wait_recv())

    def first_pieces(s):
        ia = coords[0, 0, 0, s]
        ib = coords[1, 0, 0, s]
        cur_b[s] = band_b[ib // own_b, ib % own_b]

        def from_selection():
            cur_a[s] = jnp.where(ia // own_a == c, a_ref[ia % own_a], sel_in[s])

        def from_band():
            cur_a[s] = band_a[ia // own_a, ia % own_a]

        when(at_end, from_selection)
        when(jnp.logical_not(at_end), from_band)

    loop(slots, first_pieces)

    def gradients(t, s):
        piece_a = cur_a[s]
        piece_b = cur_b[s]
        piece_c = c_ref[coords[2, 0, 0, s]]
        flag = jnp.where(s < limit, 1.0, 0.0).astype(jnp.float32)
        scaled = (piece_c[:, None, :] * piece_a[None, :, :]).reshape(depth * side, -1)
        scaled = split(scaled)
        split_b = split(piece_b)
        model = dot3(scaled, split_b, ((1,), (1,)))
        observed = counts[s].astype(jnp.float32)
        residual = split((jnp.exp(model) - observed) * flag)
        product = dot3(residual, split_b, ((1,), (0,)))
        grad_a = jnp.sum(product.reshape(depth, side, -1) * piece_c[:, None, :], axis=0)
        grad_b = dot3(residual, scaled, ((0,), (0,)))
        if t:
            grad_a = grad_a + raw_a[t - 1, c, s]
            grad_b = grad_b + raw_b[t - 1, r, s]
        raw_a[t, c, s] = grad_a
        raw_b[t, r, s] = grad_b

    def absorb(raw, tag, acc, ids, t, o):
        tags = tag[o]
        for i, block in enumerate(ids):
            match = [tags[s:s + 1, :] == block for s in range(slots)]
            total = acc[i]
            for s in range(slots):
                total = total + jnp.where(match[s], raw[t, o, s], 0.0)
            acc[i] = total

    def own_copy(t, k, o, s):
        place = raw_a.at[t, o, s]
        return remote(place, place, own_send.at[t, k], own_recv.at[t, k], toward(k))

    def own_whole(t, k, o):
        place = raw_a.at[t, o]
        return remote(place, place, own_send.at[t, k], own_recv.at[t, k], toward(k))

    def far_copy(t, k, o, q):
        place = raw_a.at[t, o, :, cut(q)]
        return remote(place, place, far_send.at[t, k, o], far_recv.at[t, o, q], toward(k))

    def wanted(t):
        return own_a if t == STEPS - 1 else slots

    def part_copy(t, k, q):
        n = wanted(t)
        return remote(part_out.at[t, k, pl.ds(0, n), cut(q)], part_in.at[t, pl.ds(0, n), cut(q)],
                      part_send.at[t, k], part_recv.at[t], toward(k))

    def part_whole(t, k):
        n = wanted(t)
        return remote(part_out.at[t, k, pl.ds(0, n)], part_in.at[t, pl.ds(0, n)],
                      part_send.at[t, k], part_recv.at[t], toward(k))

    def bunch_b(t, o, g, to, send, recv):
        place = raw_b.at[t, o, pl.ds(g * bunch, bunch)]
        return remote(place, place, send, recv, (to, c))

    def cross_send(t, s, d):
        g = s // bunch
        place = raw_b.at[t, r, s]
        return remote(place, place, rb_send.at[t, d - 1], rb_recv.at[t, r, g], (chip_peer(d), c))

    def cross_recv(t, o, g):
        return bunch_b(t, o, g, r, rb_send.at[t, 0], rb_recv.at[t, o, g])

    def pair_send(t, s):
        place = raw_b.at[t, r, s]
        return remote(place, place, pb_send.at[t, 0], pb_recv.at[t, r, s // bunch], (partner, c))

    def pair_pass(t, d, g):
        o = chip_peer(d)
        return bunch_b(t, o, g, partner, pb_send.at[t, d], pb_recv.at[t, o, g])

    def pair_recv(t, o, g):
        return bunch_b(t, o, g, r, pb_send.at[t, 0], pb_recv.at[t, o, g])

    def step(t):
        last = t == STEPS - 1

        def one(s):
            for k in range(slots):
                if t == 0:
                    when(s == k, load_counts[k].wait)
            gradients(t, s)
            when(c < end, lambda: own_copy(t, 0, c, s).start())
            when(c > 0, lambda: own_copy(t, 1, c, s).start())
            loop(chips - 1, lambda d: cross_send(t, s, d + 1).start())
            pair_send(t, s).start()

        loop(slots, one)
        if last:
            ids_a = [(c * own_a + p).astype(jnp.float32) for p in range(own_a)]
            ids_b = [(r * own_b + p).astype(jnp.float32) for p in range(own_b)]
        else:
            ids_a = [coords[0, 0, 0, s].astype(jnp.float32) for s in range(slots)]
            ids_b = [coords[1, 0, 0, s].astype(jnp.float32) for s in range(slots)]
        take_a = lambda o: absorb(raw_a, tag_a, acc_a, ids_a, t, o)
        take_b = lambda o: absorb(raw_b, tag_b, acc_b, ids_b, t, o)
        acc_a[...] = jnp.zeros_like(acc_a)
        acc_b[...] = jnp.zeros_like(acc_b)
        take_a(c)
        take_b(r)

        for k in range(2):
            o = origin_of(k, 1)

            def neighbour():
                own_whole(t, k, o).wait_recv()
                when(passes_rows(k), lambda: loop(SLICES, lambda q: far_copy(t, k, o, q).start()))

            when(inside(o), neighbour)
        for g in range(groups):
            pair_recv(t, partner, g).wait_recv()

        def part(k, q):
            there = c + 1 - 2 * k
            origins = range(0, n_col - 2) if k == 0 else range(2, n_col)
            aims = tag_a[there]
            for i in range(wanted(t)):
                if last:
                    aim = (there * own_a + i).astype(jnp.float32)
                else:
                    aim = aims[i:i + 1, :]
                total = jnp.zeros((high, a_ref.shape[2]), jnp.float32)
                for o in origins:
                    tags = tag_a[o]
                    for s in range(slots):
                        total = total + jnp.where(tags[s:s + 1, :] == aim, raw_a[t, o, s, cut(q)], 0.0)
                part_out[t, k, i, cut(q)] = total

        def far_slice(q):
            for d in range(2, n_col - 1):
                for k in range(2):
                    o = origin_of(k, d)

                    def arrived():
                        far_copy(t, k, o, q).wait_recv()
                        when(passes_rows(k), lambda: far_copy(t, k, o, q).start())

                    when(both(inside(o), takes_rows(k)), arrived)
            if n_col > 2:
                for k in range(2):
                    def summed():
                        part(k, q)
                        part_copy(t, k, q).start()

                    when(is_next_to_end(k), summed)

        loop(SLICES, far_slice)
        take_b(partner)
        for k in range(2):
            when(inside(origin_of(k, 1)), lambda: take_a(origin_of(k, 1)))

        def hand_over(d):
            for g in range(groups):
                cross_recv(t, chip_peer(d), g).wait_recv()
                pair_pass(t, d, g).start()

        loop(chips - 1, lambda d: hand_over(d + 1))
        loop(chips - 1, lambda d: take_b(chip_peer(d + 1)))

        def far_take(d):
            for k in range(2):
                o = origin_of(k, d)
                when(both(inside(o), takes_rows(k)), lambda: take_a(o))

        loop(max(n_col - 3, 0), lambda d: far_take(d + 2))
        if n_col > 2:
            def add_part():
                part_whole(t, 0).wait_recv()
                for i in range(wanted(t)):
                    acc_a[i] = acc_a[i] + part_in[t, i]

            when(at_end, add_part)

        def receive_pair(d):
            o = lax.rem(partner + 2 * d, n_row)
            for g in range(groups):
                pair_recv(t, o, g).wait_recv()
            take_b(o)

        loop(chips - 1, lambda d: receive_pair(d + 1))
        if last:
            for p in range(own_a):
                out_a[p] = a_ref[p] - step_rate * acc_a[p]
            for p in range(own_b):
                out_b[p] = b_ref[p] - step_rate * acc_b[p]
        else:
            for s in range(slots):
                cur_a[s] = cur_a[s] - step_rate * acc_a[s]
                cur_b[s] = cur_b[s] - step_rate * acc_b[s]

    for t in range(STEPS):
        step(t)

    for k in range(2):
        def sent_shard(o, k=k):
            place = band_a.at[o]
            remote(place, place, ga_send.at[k, o], ga_recv.at[o, 0], toward(k)).wait_send()

        def sent_far(t, o, k=k):
            place = raw_a.at[t, o]
            remote(place, place, far_send.at[t, k, o], far_recv.at[t, o, 0], toward(k)).wait_send()

        def sent_from(d):
            o = origin_of(k, d)
            when(both(inside(o), passes_rows(k)), lambda: sent_shard(o))

        def sent_far_from(d):
            o = origin_of(k, d)
            for t in range(STEPS):
                when(both(inside(o), passes_rows(k)), lambda: sent_far(t, o))

        loop(n_col - 1, sent_from)
        loop(n_col - 2, lambda d: sent_far_from(d + 1))
        when(is_next_to_end(k),
             lambda: remote(sel_out.at[k], sel_in, sel_send.at[k], sel_recv.at[0], toward(k)).wait_send())
        for t in range(STEPS):
            when(c < end if k == 0 else c > 0, lambda: own_whole(t, k, c).wait_send())
            if n_col > 2:
                when(is_next_to_end(k), lambda: part_whole(t, k).wait_send())
    loop(n_row - 1, lambda d: gather_b(r, d + 1).wait_send())
    loop(n_col - 1, lambda d: tag_copy_a(c, d + 1).wait_send())
    loop(n_row - 1, lambda d: tag_copy_b(r, d + 1).wait_send())
    for t in range(STEPS):
        place = raw_b.at[t, r]
        loop(chips - 1, lambda d: remote(
            place, place, rb_send.at[t, d], rb_recv.at[t, r, 0], (chip_peer(d + 1), c)).wait_send())
        loop(chips, lambda d: remote(
            place, place, pb_send.at[t, d], pb_recv.at[t, r, 0], (partner, c)).wait_send())


def local(n_row, n_col, counts, block_coords, block_count, factor_a, factor_b, factor_c):
    slots, depth, side = counts.shape[2:5]
    rank = factor_a.shape[1]
    own_a = factor_a.shape[0] // side
    own_b = factor_b.shape[0] // side
    chips = n_row // 2
    lines = -(-slots // 8) * 8
    groups = 2 if slots % 2 == 0 else 1
    most = max(slots, own_a)
    f32 = jnp.float32
    vmem = pl.BlockSpec(memory_space=pltpu.VMEM)
    smem = pl.BlockSpec(memory_space=pltpu.SMEM)
    dma = pltpu.SemaphoreType.DMA
    out_a, out_b = pl.pallas_call(
        functools.partial(kernel, n_row, n_col),
        out_shape=(
            jax.ShapeDtypeStruct((own_a, side, rank), f32),
            jax.ShapeDtypeStruct((own_b, side, rank), f32),
        ),
        in_specs=[smem, smem, vmem, vmem, vmem, pl.BlockSpec(memory_space=pl.ANY)],
        out_specs=(vmem, vmem),
        scratch_shapes=[
            pltpu.VMEM((slots, depth * side, side), jnp.int32),
            pltpu.VMEM((n_col, own_a, side, rank), f32),
            pltpu.VMEM((n_row, own_b, side, rank), f32),
            pltpu.VMEM((2, slots, side, rank), f32),
            pltpu.VMEM((slots, side, rank), f32),
            pltpu.VMEM((slots, side, rank), f32),
            pltpu.VMEM((slots, side, rank), f32),
            pltpu.VMEM((STEPS, n_col, slots, side, rank), f32),
            pltpu.VMEM((STEPS, n_row, slots, side, rank), f32),
            pltpu.VMEM((STEPS, 2, most, side, rank), f32),
            pltpu.VMEM((STEPS, most, side, rank), f32),
            pltpu.VMEM((n_col, lines, rank), f32),
            pltpu.VMEM((n_row, lines, rank), f32),
            pltpu.VMEM((most, side, rank), f32),
            pltpu.VMEM((max(slots, own_b), side, rank), f32),
            dma((slots,)),
            dma((2, n_col)),
            dma((n_col, SLICES)),
            dma((2,)),
            dma((1,)),
            dma((n_row - 1,)),
            dma((n_row,)),
            dma((STEPS, 2)),
            dma((STEPS, 2)),
            dma((STEPS, 2, n_col)),
            dma((STEPS, n_col, SLICES)),
            dma((STEPS, 2)),
            dma((STEPS,)),
            dma((STEPS, chips - 1)),
            dma((STEPS, n_row, groups)),
            dma((STEPS, chips)),
            dma((STEPS, n_row, groups)),
            dma((n_col - 1,)),
            dma((n_col,)),
            dma((n_row - 1,)),
            dma((n_row,)),
        ],
        compiler_params=pltpu.CompilerParams(
            collective_id=0, has_side_effects=True, vmem_limit_bytes=56 * 1024 * 1024
        ),
    )(
        block_coords,
        block_count,
        factor_a.reshape(own_a, side, rank),
        factor_b.reshape(own_b, side, rank),
        factor_c.reshape(-1, depth, rank),
        counts.reshape(slots, depth * side, side),
    )
    return out_a.reshape(factor_a.shape), out_b.reshape(factor_b.shape)


def solution(mesh):
    n_row = mesh.shape["row"]
    n_col = mesh.shape["col"]
    return jax.shard_map(
        functools.partial(local, n_row, n_col),
        mesh=mesh,
        in_specs=(
            P("row", "col", None, None, None, None),
            P(None, "row", "col", None),
            P("row", "col"),
            P(("row", "col"), None),
            P(("col", "row"), None),
            P(),
        ),
        out_specs=(P(("row", "col"), None), P(("col", "row"), None)),
        check_vma=False,
    )
```
